32 devices in a mesh: section: 2 (over x), row: 4 (over z), col: 4 (over y, core).
Axes of the slice: x: 2, y: 2, z: 4, core: 2. Of those that a mesh axis runs over, the one named last changes fastest.
Arguments:
- streams: bfloat16 [2, 1024, 6144], P('section', 'col', 'row'), may hold values from -6 to 6
- tiles: bfloat16 [2, 6144, 24576], P('section', 'row', 'col'), may hold values from -0.078125 to 0.078125
- order: int32 [8], replicated, may hold values from 0 to 7, each once
Outputs:
- result: bfloat16 [2, 1024, 6144], P('section', 'col', 'row')
The draws below stay inside these ranges and needn't reach their ends.
Inputs may be any that keep to these rules, and one draw needn't show every extreme that they name: order names every block number once.
All inputs are finite; a program needn't handle non-finite values.
Results may differ from the reference program's by a relative error of at most 0.0054.
Values may be sent and summed in bfloat16 or wider, within the bound.
No kernel may reach another device: no remote copies, remote signals or barrier semaphores. Data moves between devices by JAX's collectives and lax.ppermute only.
A program may use at most 256 MiB of HBM per device.

```python
import jax
import jax.numpy as jnp

D = 6144
F = 24576
ROWS = 1024
BLOCKS = 8


def level_of(key, shape, pieces, smallest, largest):
    loudness = 1.0
    for dim, blocks in pieces:
        draws = jax.random.uniform(jax.random.fold_in(jax.random.fold_in(key, 6), dim), (blocks,), jnp.float32, smallest / len(pieces), largest / len(pieces))
        loudness = loudness * jnp.repeat(jnp.exp(draws), shape[dim] // blocks).reshape((-1,) + (1,) * (len(shape) - 1 - dim))
    return loudness


def scatter_about(rng, dims, scale, reach, pieces=(), held_as=jnp.bfloat16):
    array = jax.random.normal(rng, dims, jnp.float32) * scale
    if len(pieces) > 0:
        array = level_of(rng, dims, pieces, -0.22, 0.18) * array
    return jnp.clip(array, min=-reach, max=reach).astype(held_as)


def setup_inputs(seed: int = 0) -> dict:
    arg_keys = jax.random.split(jax.random.key(seed), 4)
    return {
        "streams": scatter_about(arg_keys[0], (2, ROWS, D), 1.0, 6.0, ((0, 2), (1, 4), (2, 4))),
        "tiles": scatter_about(arg_keys[1], (2, D, F), D ** -0.5, 0.078125, ((0, 2), (1, 4), (2, 4))),
        "order": jax.random.permutation(arg_keys[2], BLOCKS).astype(jnp.int32),
    }


gelu_scale = 0.7978845608
gelu_cubic = 0.044715


def gelu_value(v):
    inner = jnp.tanh(gelu_scale * (v + gelu_cubic * v * v * v))
    return 0.5 * v * (1.0 + inner)


def gelu_slope(v):
    inner = jnp.tanh(gelu_scale * (v + gelu_cubic * v * v * v))
    return 0.5 * (1.0 + inner) + 0.5 * v * (1.0 - inner * inner) * gelu_scale * (1.0 + 3.0 * gelu_cubic * v * v)


def reorder(rows, index):
    shaped = rows.reshape(BLOCKS, 128, rows.shape[1])
    return jnp.take(shaped, index, axis=0).reshape(rows.shape)


def reference(streams, tiles, order):
    inputs = streams[0]
    cotangent = streams[1]
    w_up = tiles[0]
    w_down_t = tiles[1]
    counter = jnp.arange(BLOCKS, dtype=jnp.int32)
    inverse = jnp.sum(jnp.where(order[None, :] == counter[:, None], counter[None, :], 0), axis=1).astype(jnp.int32)
    pre = jnp.dot(inputs, w_up, preferred_element_type=jnp.float32)
    hidden = gelu_value(pre).astype(jnp.bfloat16)
    forward = jnp.dot(reorder(hidden, order), w_down_t.T, preferred_element_type=jnp.float32).astype(jnp.bfloat16)
    back_b = jnp.dot(cotangent, w_down_t, preferred_element_type=jnp.float32)
    back = reorder(back_b, inverse).astype(jnp.bfloat16)
    slope = (back.astype(jnp.float32) * gelu_slope(pre)).astype(jnp.bfloat16)
    grad_in = jnp.dot(slope, w_up.T, preferred_element_type=jnp.float32).astype(jnp.bfloat16)
    return jnp.stack([grad_in, forward])
```

```python
import jax
import jax.numpy as jnp
from jax import lax
from jax.sharding import PartitionSpec as P

gelu_scale = 0.7978845608
gelu_cubic = 0.044715
COLUMN_CHUNKS = 4
TOKEN_GROUPS = 4
SKEW = 2


def partner(value, axis, bit):
    mask = 2**bit
    pairs = [(source, source ^ mask) for source in range(lax.axis_size(axis))]
    return lax.ppermute(value, axis, pairs)


def gelu_value(v):
    inner = jnp.tanh(gelu_scale * (v + gelu_cubic * v * v * v))
    return 0.5 * v * (1.0 + inner)


def gelu_slope(v):
    inner = jnp.tanh(gelu_scale * (v + gelu_cubic * v * v * v))
    return 0.5 * (1.0 + inner) + 0.5 * v * (1.0 - inner * inner) * gelu_scale * (
        1.0 + 3.0 * gelu_cubic * v * v
    )


def gather_rows(own, bits):
    shards, masks = [own], [0]
    for bit in reversed(range(bits)):
        shards = shards + [partner(shard, "col", bit) for shard in shards]
        masks = masks + [mask ^ (1 << bit) for mask in masks]
    return shards, masks


def scatter_sum(partials, col, bits):
    held = partials
    for bit in range(bits):
        pairs = held.reshape(held.shape[0] // 2, 2, *held.shape[1:])
        mine = (col >> bit) & 1
        keep = jnp.where(mine == 0, pairs[:, 0], pairs[:, 1])
        give = jnp.where(mine == 0, pairs[:, 1], pairs[:, 0])
        if bit > 0:
            give = give.astype(jnp.bfloat16)
        held = keep + partner(give, "col", bit).astype(jnp.float32)
    return held[0]


def per_device(streams, tiles, order):
    row_size, col_size = lax.axis_size("row"), lax.axis_size("col")
    row, col = lax.axis_index("row"), lax.axis_index("col")
    first_section = lax.axis_index("section") == 0
    bits = col_size.bit_length() - 1
    own_rows, weight = streams[0], tiles[0]
    local, depth = own_rows.shape
    tokens = local * col_size
    half = weight.shape[1] // 2
    chunks, groups = COLUMN_CHUNKS, TOKEN_GROUPS
    chunk = half // chunks
    group_rows = tokens // groups
    unit = local // groups
    block = tokens // order.shape[0]
    last = row_size - 1

    shards, masks = gather_rows(own_rows, bits)
    place = [masks.index(g) for g in range(col_size)]
    place = jnp.array(place, jnp.int32)
    per_block = block // unit
    counter = jnp.arange(order.shape[0], dtype=jnp.int32)
    inverse = jnp.sum(jnp.where(order[None, :] == counter[:, None], counter[None, :], 0), axis=1)
    moved = jnp.where(first_section, inverse, order)
    units = jnp.arange(tokens // unit, dtype=jnp.int32)
    source = jnp.take(moved, units // per_block) * per_block + units % per_block

    def position(index):
        return jnp.take(place, (index // groups) ^ col) * groups + index % groups

    own_place, other_place = position(units), position(source)

    each = col_size // groups
    if each > 1:
        grouped = [jnp.concatenate(shards[i * each : (i + 1) * each]) for i in range(groups)]
    else:
        grouped = shards
    stacked = jnp.stack(grouped)

    pieces = [(0, j) for j in range(chunks)]
    pieces += [(g, j) for j in range(chunks) for g in range(1, groups)]
    count = len(pieces)
    group_of = jnp.array([g for g, _ in pieces], jnp.int32)
    chunk_of = jnp.array([j for _, j in pieces], jnp.int32)
    sends = [(t, j) for j in range(chunks // 2) for t in range(groups)]
    sends += [(t, j) for t in range(groups) for j in range(chunks // 2, chunks)]
    right = [(d, d + 1) for d in range(last)]
    left = [(d + 1, d) for d in range(last)]

    def partial_sum(slot, start, offset):
        index = jnp.clip(slot - start, 0, count - 1)
        if slot < chunks:
            rows = grouped[0]
        else:
            rows = lax.dynamic_index_in_dim(stacked, group_of[index], 0, keepdims=False)
        columns = lax.dynamic_slice_in_dim(weight, offset + chunk_of[index] * chunk, chunk, 1)
        sums = jnp.dot(rows, columns, preferred_element_type=jnp.float32)
        if slot >= count:
            sums = jnp.where(slot - start < count, sums, 0.0)
        return sums

    starts = (SKEW * row, SKEW * (last - row))
    ends = (row == 0, row == last)
    offsets = (0, half)
    paths = (right, left)
    arrived = ({}, {})
    held = ({}, {})
    pre, incoming, mixed = {}, {}, {}
    depth_slots = SKEW * last
    ready = [max(i for i, (_, k) in enumerate(pieces) if k == j) for j in range(chunks)]
    back = max(depth_slots + ready[j] + 2 - i for i, (_, j) in enumerate(sends))
    back = max(back, count)
    slots = back + count + depth_slots
    product = [None] * groups
    finished = [None] * groups

    def mix(j):
        theirs = jnp.concatenate([incoming[pieces.index((g, j))] for g in range(groups)])
        theirs = theirs.reshape(-1, unit, chunk)
        ours = jnp.concatenate([pre[pieces.index((g, j))] for g in range(groups)])
        ours = ours.reshape(-1, unit, chunk)
        for t in range(groups):
            a = jnp.take(theirs, other_place[t::groups], axis=0).astype(jnp.float32)
            v = jnp.take(ours, own_place[t::groups], axis=0)
            m = jnp.where(first_section, a * gelu_slope(v), a).astype(jnp.bfloat16)
            mixed[(t, j)] = m.reshape(group_rows, chunk)

    for slot in range(slots):
        totals = [None, None]
        for way in range(2):
            base = arrived[way].get(slot - SKEW)
            if back <= slot < back + count:
                base = jnp.where(ends[way], mixed[sends[slot - back]], base)
            if slot < count + depth_slots:
                sums = partial_sum(slot, starts[way], offsets[way])
                if base is not None:
                    sums = base.astype(jnp.float32) + sums
                totals[way] = sums
                base = sums.astype(jnp.bfloat16)
            held[way][slot] = base
            if slot < slots - SKEW:
                arrived[way][slot] = lax.ppermute(base, "row", paths[way])
        index = slot - depth_slots
        if 0 <= index < count:
            total = jnp.where(row == 0, totals[1], totals[0])
            pre[index] = total
            outgoing = jnp.where(first_section, gelu_value(total), total).astype(jnp.bfloat16)
            incoming[index] = partner(outgoing, "section", 0)
            for j in range(chunks):
                if index == ready[j]:
                    mix(j)
        index = slot - depth_slots - back
        if index >= 0:
            t, j = sends[index]
            for way in range(2):
                value = held[way][back + index + SKEW * last]
                for d in range(last):
                    ahead = SKEW * (d if way == 0 else d)
                    here = row == (d if way == 0 else last - d)
                    value = jnp.where(here, held[way][back + index + ahead], value)
                begin = offsets[1 - way] + j * chunk
                term = lax.dot_general(
                    value,
                    weight[:, begin : begin + chunk],
                    (((1,), (1,)), ((), ())),
                    preferred_element_type=jnp.float32,
                )
                product[t] = term if product[t] is None else product[t] + term
            if index == max(i for i, (u, _) in enumerate(sends) if u == t):
                parts = product[t].reshape(col_size, unit, depth)
                finished[t] = scatter_sum(parts, col, bits).astype(jnp.bfloat16)
    return jnp.concatenate(finished)[None]


def solution(mesh):
    placed = (P("section", "col", "row"), P("section", "row", "col"), P())
    return jax.shard_map(
        per_device,
        mesh=mesh,
        in_specs=placed,
        out_specs=P("section", "col", "row"),
        check_vma=False,
    )
```

```python
import functools

import jax
import jax.numpy as jnp
from jax import lax
from jax.experimental import pallas as pl
from jax.experimental.pallas import tpu as pltpu
from jax.sharding import PartitionSpec as P

gelu_scale = 0.7978845608
gelu_cubic = 0.044715
COLUMN_CHUNKS = 3
TOKEN_GROUPS = 4
TILES = (512, 256, 128)
VMEM_BYTES = 40 * 2**20


def partner(value, axis, bit):
    mask = 2**bit
    pairs = [(source, source ^ mask) for source in range(lax.axis_size(axis))]
    return lax.ppermute(value, axis, pairs)


def gather_rows(own, bits, later):
    shards, masks = [own], [0]
    for bit in reversed(range(bits)):
        arrived = [partner(shard, "col", bit) for shard in shards]
        if bit > 0:
            arrived = list(lax.optimization_barrier((*arrived, later)))[:-1]
        shards, masks = shards + arrived, masks + [mask ^ (1 << bit) for mask in masks]
    return shards, masks


def tile_of(chunk):
    return next(tile for tile in TILES if chunk % tile == 0)


class Chain:
    def __init__(self):
        self.value = None

    def call(self, kernel, specs, operands, **kwargs):
        extra = 0 if self.value is None else 1
        prefetch = kwargs["prefetch"]
        skip = prefetch + len(specs)

        def body(*refs):
            kernel(*refs[:skip], *refs[skip + extra :])

        outs = pl.pallas_call(
            body,
            grid_spec=pltpu.PrefetchScalarGridSpec(
                num_scalar_prefetch=prefetch,
                grid=kwargs["grid"],
                in_specs=specs + [pl.BlockSpec(memory_space=pl.ANY)] * extra,
                out_specs=kwargs["out_specs"],
                scratch_shapes=kwargs.get("scratch", ()),
            ),
            out_shape=kwargs["out_shape"],
            compiler_params=pltpu.CompilerParams(vmem_limit_bytes=VMEM_BYTES),
            cost_estimate=pl.CostEstimate(flops=1, bytes_accessed=1, transcendentals=0),
        )(*operands, *([self.value] if extra else []))
        self.value = outs[0]
        return outs


def scatter_sum(partials, col, bits):
    held = partials
    for bit in range(bits):
        pairs = held.reshape(held.shape[0] // 2, 2, *held.shape[1:])
        mine = (col >> bit) & 1
        keep = jnp.where(mine == 0, pairs[:, 0], pairs[:, 1])
        give = jnp.where(mine == 0, pairs[:, 1], pairs[:, 0])
        if bit > 0:
            give = give.astype(jnp.bfloat16)
        held = keep + partner(give, "col", bit).astype(jnp.float32)
    return held[0]


def piece_of(index, chunks, groups):
    rest = jnp.maximum(index - chunks, 0)
    first = index < chunks
    group = jnp.where(first, 0, 1 + lax.rem(rest, groups - 1))
    return group, jnp.where(first, index, lax.div(rest, groups - 1))


def piece_kernel(live, with_base, with_total, info, rows_ref, columns_ref, *rest):
    if with_base:
        base_ref, *rest = rest
    send_ref = rest[0]
    sums = jnp.dot(rows_ref[0], columns_ref[...], preferred_element_type=jnp.float32)
    sums = jnp.where(live(info[0]), sums, 0.0)
    if with_base:
        sums = sums + base_ref[...].astype(jnp.float32)
    send_ref[...] = sums.astype(send_ref.dtype)
    if with_total:
        out_ref, slope_ref = rest[1:]

        @pl.when(info[1] == 0)
        def _():
            v = sums
            inner = jnp.tanh(gelu_scale * (v + gelu_cubic * v * v * v))
            out_ref[...] = (0.5 * v * (1.0 + inner)).astype(out_ref.dtype)
            slope_ref[...] = 0.5 * (1.0 + inner) + 0.5 * v * (1.0 - inner * inner) * gelu_scale * (
                1.0 + 3.0 * gelu_cubic * v * v
            )

        @pl.when(info[1] != 0)
        def _():
            out_ref[...] = sums.astype(out_ref.dtype)
            slope_ref[...] = jnp.ones_like(slope_ref)


def piece_sum(chain, info, rows, weight, base, index, upper, count, chunks, with_total):
    groups, group_rows, depth = rows.shape
    chunk = weight.shape[1] // (2 * chunks)
    tile = tile_of(chunk)
    tiles = chunk // tile

    def which(info):
        return piece_of(jnp.clip(index(info[0]), 0, count - 1), chunks, TOKEN_GROUPS)

    def rows_map(t, info):
        return (which(info)[0] if groups > 1 else 0, 0, 0)

    def columns_map(t, info):
        return (0, (upper(info[0]) * chunks + which(info)[1]) * tiles + t)

    piece = pl.BlockSpec((group_rows, tile), lambda t, info: (0, t))
    in_specs = [
        pl.BlockSpec((1, group_rows, depth), rows_map),
        pl.BlockSpec((depth, tile), columns_map),
    ]
    operands = [info, rows, weight]
    if base is not None:
        in_specs.append(piece)
        operands.append(base)
    shape = (group_rows, chunk)
    outs = [jax.ShapeDtypeStruct(shape, jnp.bfloat16)]
    if with_total:
        outs += [jax.ShapeDtypeStruct(shape, jnp.bfloat16), jax.ShapeDtypeStruct(shape, jnp.float32)]

    def live(row):
        return index(row) < count

    return chain.call(
        functools.partial(piece_kernel, live, base is not None, with_total),
        in_specs,
        operands,
        prefetch=1,
        grid=(tiles,),
        out_specs=[piece] * len(outs),
        out_shape=outs,
    )


def choose_kernel(ends, info, here_ref, there_ref, out_ref):
    out_ref[...] = jnp.where(ends(info[0]), here_ref[...], there_ref[...])


def choose(chain, info, ends, here, there):
    size, chunk = here.shape
    tile = chunk // 2 if chunk % 256 == 0 else chunk
    piece = pl.BlockSpec((size, tile), lambda t, info: (0, t))
    return chain.call(
        functools.partial(choose_kernel, ends),
        [piece, piece],
        [info, here, there],
        prefetch=1,
        grid=(chunk // tile,),
        out_specs=[piece],
        out_shape=[jax.ShapeDtypeStruct(here.shape, here.dtype)],
    )[0]


def mix_kernel(groups, unit, info, ours_at, theirs_at, *refs):
    theirs, slopes = refs[:groups], refs[groups : 2 * groups]
    outs = refs[2 * groups : 3 * groups]
    their_rows, slope_rows = refs[3 * groups :]
    size = theirs[0].shape[0]
    for g in range(groups):
        their_rows[g * size : (g + 1) * size, :] = theirs[g][...]
        slope_rows[g * size : (g + 1) * size, :] = slopes[g][...]
    for k in range(groups * size // unit):
        a = their_rows[pl.ds(pl.multiple_of(theirs_at[k] * unit, unit), unit), :].astype(jnp.float32)
        b = slope_rows[pl.ds(pl.multiple_of(ours_at[k] * unit, unit), unit), :]
        where = k // groups * unit
        outs[k % groups][where : where + unit, :] = (a * b).astype(jnp.bfloat16)


def mix(chain, info, ours_at, theirs_at, theirs, slopes, unit):
    groups = len(theirs)
    size, chunk = theirs[0].shape
    tile = min(256, tile_of(chunk))
    piece = pl.BlockSpec((size, tile), lambda t, *_: (0, t))
    return chain.call(
        functools.partial(mix_kernel, groups, unit),
        [piece] * (2 * groups),
        [info, ours_at, theirs_at, *theirs, *slopes],
        prefetch=3,
        grid=(chunk // tile,),
        out_specs=[piece] * groups,
        out_shape=[jax.ShapeDtypeStruct((size, chunk), jnp.bfloat16)] * groups,
        scratch=[
            pltpu.VMEM((groups * size, tile), jnp.bfloat16),
            pltpu.VMEM((groups * size, tile), jnp.float32),
        ],
    )


def product_kernel(hops, members, with_base, info, *refs):
    out_ref = refs[-1]
    values = refs[: hops * members]
    lower_ref, upper_ref = refs[hops * members : hops * members + 2]
    step, row, last = pl.program_id(0), info[0], hops - 1
    size = values[0].shape[0]
    dims = (((1,), (1,)), ((), ()))
    for m in range(members):
        stages = values[m * hops : (m + 1) * hops]
        upper_value, lower_value = stages[0][...], stages[last][...]
        for d in range(1, last + 1):
            upper_value = jnp.where(row == d, stages[d][...], upper_value)
            lower_value = jnp.where(row == d, stages[last - d][...], lower_value)
        term = lax.dot_general(lower_value, lower_ref[...], dims, preferred_element_type=jnp.float32)
        term += lax.dot_general(upper_value, upper_ref[...], dims, preferred_element_type=jnp.float32)
        here = pl.ds(m * size, size)

        @pl.when(step == 0)
        def _(term=term, here=here):
            out_ref[here, :] = term + refs[-2][here, :] if with_base else term

        @pl.when(step > 0)
        def _(term=term, here=here):
            out_ref[here, :] += term


def product_sum(chain, info, stages, weight, base, base_at, j, chunks):
    members, hops = len(stages), len(stages[0])
    size, chunk = stages[0][0].shape
    depth = weight.shape[0]
    tile = tile_of(chunk)
    tiles = chunk // tile
    piece = pl.BlockSpec((size, tile), lambda t, info: (0, t))
    in_specs = [piece] * (members * hops)
    in_specs += [
        pl.BlockSpec((depth, tile), lambda t, info: (0, j * tiles + t)),
        pl.BlockSpec((depth, tile), lambda t, info: (0, (chunks + j) * tiles + t)),
    ]
    operands = [info, *[value for member in stages for value in member], weight, weight]
    if base is not None:
        in_specs.append(pl.BlockSpec((members * size, depth), lambda t, info: (base_at, 0)))
        operands.append(base)
    return chain.call(
        functools.partial(product_kernel, hops, members, base is not None),
        in_specs,
        operands,
        prefetch=1,
        grid=(tiles,),
        out_specs=[pl.BlockSpec((members * size, depth), lambda t, info: (0, 0))],
        out_shape=[jax.ShapeDtypeStruct((members * size, depth), jnp.float32)],
    )[0]


def per_device(streams, tiles, order):
    row_size, col_size = lax.axis_size("row"), lax.axis_size("col")
    row, col = lax.axis_index("row"), lax.axis_index("col")
    section = lax.axis_index("section")
    bits = col_size.bit_length() - 1
    own_rows, weight = streams[0], tiles[0]
    local, depth = own_rows.shape
    tokens = local * col_size
    chunks, groups = COLUMN_CHUNKS, TOKEN_GROUPS
    group_rows = tokens // groups
    unit = local // groups
    last = row_size - 1
    info = jnp.stack([row, section]).astype(jnp.int32)

    each = col_size // groups
    per_block = tokens // order.shape[0] // unit
    counter = jnp.arange(order.shape[0], dtype=jnp.int32)
    inverse = jnp.sum(jnp.where(order[None, :] == counter[:, None], counter[None, :], 0), axis=1)
    moved = jnp.where(section == 0, inverse, order)
    units = jnp.arange(tokens // unit, dtype=jnp.int32)
    source = (moved[:, None] * per_block + jnp.arange(per_block, dtype=jnp.int32)).reshape(-1)

    def position(index):
        shard, found = (index // groups) ^ col, 0
        for bit in range(bits):
            found = found | (((shard >> bit) & 1) << (bits - 1 - bit))
        return (found * groups + index % groups).astype(jnp.int32)

    ours_at, theirs_at = position(units), position(source)

    even = [(d, d ^ 1) for d in range(row_size)]
    odd = [(d, ((d - 1) ^ 1) + 1) for d in range(1, last)]
    count = groups * chunks
    pieces = [(0, j) for j in range(chunks)]
    pieces += [(g, j) for j in range(chunks) for g in range(1, groups)]
    span = 3 * (row_size - 2) // 2
    ready = [max(i for i, (_, k) in enumerate(pieces) if k == j) for j in range(chunks)]
    sends = [(t, j) for j in range(chunks) for t in range(groups)]
    back = max(ready[j] + span + 4 - i for i, (_, j) in enumerate(sends))
    back = max(back, count)
    final = back + count - 1
    even_slots = final + span + 1
    odd_slots = range(1, final + 2 + 3 * (row_size - 4) // 2)

    def first_index(slot, r):
        q = jnp.where(r % 2 == 1, r, last - r)
        return slot - 3 * ((q - 1) // 2)

    def second_index(slot, r):
        q = jnp.where(r % 2 == 0, r, last - r)
        return slot + 2 - 3 * (q // 2)

    def first_half(r):
        return 1 - r % 2

    def second_half(r):
        return r % 2

    def gathered(later):
        shards, masks = gather_rows(own_rows, bits, later)
        if each > 1:
            shards = [jnp.concatenate(shards[i * each : (i + 1) * each]) for i in range(groups)]
        return jnp.stack(shards)

    def rows_for(newest):
        if each == 1 and newest < chunks:
            return own_rows[None]
        if not whole_rows:
            whole_rows.append(gathered(chain.value if chain.value is not None else own_rows))
        return whole_rows[0]

    def at_end(r):
        return (r == 0) | (r == last)

    def is_live(index):
        return 0 <= index < count

    chain, whole_rows = Chain(), []
    even_send, odd_send, even_got, odd_got = {}, {}, {}, {}
    incoming, slopes, mixed, waiting = {}, {}, {}, []
    sums, finished = {}, [None] * groups

    def second(slot):
        base = odd_got.get(slot)
        newest = slot + 2
        if 0 <= newest - back < count:
            value = mixed[sends[newest - back]]
            base = value if base is None else choose(chain, info, at_end, value, base)
        if any(is_live(newest - 3 * (q // 2)) for q in range(0, last, 2)):
            (base,) = piece_sum(
                chain, info, rows_for(newest), weight, base,
                functools.partial(second_index, slot), second_half, count, chunks, False,
            )
        even_send[newest] = base

    def first(slot):
        base = even_got[slot]
        total = is_live(slot - span)
        passes = any(is_live(slot - 3 * ((q - 1) // 2)) for q in range(1, last, 2))
        odd_send[slot + 1] = base
        if total or passes:
            send, *rest = piece_sum(
                chain, info, rows_for(slot), weight, base,
                functools.partial(first_index, slot), first_half, count, chunks, total,
            )
            if passes:
                odd_send[slot + 1] = send
            if total:
                outgoing, slopes[slot - span] = rest
                incoming[slot - span] = partner(outgoing, "section", 0)

    second(-2)
    second(-1)
    even_got[0] = lax.ppermute(even_send[0], "row", even)
    for slot in range(even_slots):
        if slot + 1 < even_slots:
            even_got[slot + 1] = lax.ppermute(even_send[slot + 1], "row", even)
        first(slot)
        if slot + 1 in odd_slots:
            odd_got[slot + 1] = lax.ppermute(odd_send[slot + 1], "row", odd)
        for j in range(chunks):
            if slot == ready[j] + span + 2:
                found = [pieces.index((g, j)) for g in range(groups)]
                parts = mix(
                    chain, info, ours_at, theirs_at, [incoming[i] for i in found], [slopes[i] for i in found], unit
                )
                mixed.update({(t, j): part for t, part in enumerate(parts)})
        b = slot - span - back
        if b >= 0:
            t, j = sends[b]
            index = back + b
            stages = [mixed[(t, j)]]
            for q in range(1, row_size):
                if q % 2 == 1:
                    stages.append(even_got[index + 3 * ((q - 1) // 2)])
                else:
                    stages.append(odd_got[index - 2 + 3 * (q // 2)])
            waiting.append(stages)
            if j < chunks - 1 and t % 2 == 1:
                sums[t // 2] = product_sum(chain, info, waiting, weight, sums.get(t // 2), 0, j, chunks)
                waiting = []
            if j == chunks - 1:
                parts = product_sum(chain, info, waiting, weight, sums[t // 2], t % 2, j, chunks)
                waiting = []
                parts = parts.reshape(col_size, unit, depth)
                finished[t] = scatter_sum(parts, col, bits).astype(jnp.bfloat16)
        if slot + 2 < even_slots:
            second(slot)
    return jnp.concatenate(finished)[None]


def solution(mesh):
    placed = (P("section", "col", "row"), P("section", "row", "col"), P())
    return jax.shard_map(
        per_device,
        mesh=mesh,
        in_specs=placed,
        out_specs=P("section", "col", "row"),
        check_vma=False,
    )
```

```python
import functools

import jax
import jax.numpy as jnp
from jax import lax
from jax.experimental import pallas as pl
from jax.experimental.pallas import tpu as pltpu
from jax.sharding import PartitionSpec as P

gelu_scale = 0.7978845608
gelu_cubic = 0.044715
COLUMN_CHUNKS = 3
TOKEN_GROUPS = 4
TILES = (512, 256, 128)
VMEM_BYTES = 47 * 2**20
COST = 0.3


def partner(value, axis, bit):
    mask = 2**bit
    pairs = [(source, source ^ mask) for source in range(lax.axis_size(axis))]
    return lax.ppermute(value, axis, pairs)


def gather_rows(own, bits, later):
    shards, masks = [own], [0]
    for bit in reversed(range(bits)):
        arrived = [partner(shard, "col", bit) for shard in shards]
        if bit > 0:
            arrived = list(lax.optimization_barrier((*arrived, later)))[:-1]
        shards, masks = shards + arrived, masks + [mask ^ (1 << bit) for mask in masks]
    return shards, masks


def tile_of(chunk):
    return next(tile for tile in TILES if chunk % tile == 0)


class Chain:
    def __init__(self):
        self.value = None
        self.watch = []

    def call(self, kernel, specs, operands, **kwargs):
        earlier = ([] if self.value is None else [self.value]) + self.watch
        extra, self.watch = len(earlier), []
        prefetch = kwargs["prefetch"]
        skip = prefetch + len(specs)

        def body(*refs):
            kernel(*refs[:skip], *refs[skip + extra :])

        outs = pl.pallas_call(
            body,
            grid_spec=pltpu.PrefetchScalarGridSpec(
                num_scalar_prefetch=prefetch,
                grid=kwargs["grid"],
                in_specs=specs + [pl.BlockSpec(memory_space=pl.ANY)] * extra,
                out_specs=kwargs["out_specs"],
                scratch_shapes=kwargs.get("scratch", ()),
            ),
            out_shape=kwargs["out_shape"],
            compiler_params=pltpu.CompilerParams(vmem_limit_bytes=VMEM_BYTES),
            cost_estimate=pl.CostEstimate(flops=int(COST * kwargs["cost"][0]) + 1, bytes_accessed=int(COST * kwargs["cost"][1]) + 1, transcendentals=0),
        )(*operands, *earlier)
        self.value = outs[0]
        return outs


def scatter_sum(partials, col, bits):
    held = partials
    for bit in range(bits):
        pairs = held.reshape(held.shape[0] // 2, 2, *held.shape[1:])
        mine = (col >> bit) & 1
        keep = jnp.where(mine == 0, pairs[:, 0], pairs[:, 1])
        give = jnp.where(mine == 0, pairs[:, 1], pairs[:, 0])
        if bit > 0:
            give = give.astype(jnp.bfloat16)
        held = keep + partner(give, "col", bit).astype(jnp.float32)
    return held[0]


def piece_of(index, chunks, groups):
    rest = jnp.maximum(index - chunks, 0)
    first = index < chunks
    group = jnp.where(first, 0, 1 + lax.rem(rest, groups - 1))
    return group, jnp.where(first, index, lax.div(rest, groups - 1))


def piece_kernel(live, with_base, with_total, info, rows_ref, columns_ref, *rest):
    if with_base:
        base_ref, *rest = rest
    send_ref = rest[0]
    sums = jnp.dot(rows_ref[0], columns_ref[...], preferred_element_type=jnp.float32)
    sums = jnp.where(live(info[0]), sums, 0.0)
    if with_base:
        sums = sums + base_ref[...].astype(jnp.float32)
    send_ref[...] = sums.astype(send_ref.dtype)
    if with_total:
        out_ref, slope_ref = rest[1:]

        @pl.when(info[1] == 0)
        def _():
            v = sums
            inner = jnp.tanh(gelu_scale * (v + gelu_cubic * v * v * v))
            out_ref[...] = (0.5 * v * (1.0 + inner)).astype(out_ref.dtype)
            slope_ref[...] = 0.5 * (1.0 + inner) + 0.5 * v * (1.0 - inner * inner) * gelu_scale * (
                1.0 + 3.0 * gelu_cubic * v * v
            )

        @pl.when(info[1] != 0)
        def _():
            out_ref[...] = sums.astype(out_ref.dtype)
            slope_ref[...] = jnp.ones_like(slope_ref)


def piece_sum(chain, info, rows, weight, base, index, upper, count, chunks, with_total):
    groups, group_rows, depth = rows.shape
    chunk = weight.shape[1] // (2 * chunks)
    tile = tile_of(chunk)
    tiles = chunk // tile

    def which(info):
        return piece_of(jnp.clip(index(info[0]), 0, count - 1), chunks, TOKEN_GROUPS)

    def rows_map(t, info):
        return (which(info)[0] if groups > 1 else 0, 0, 0)

    def columns_map(t, info):
        return (0, (upper(info[0]) * chunks + which(info)[1]) * tiles + t)

    piece = pl.BlockSpec((group_rows, tile), lambda t, info: (0, t))
    in_specs = [
        pl.BlockSpec((1, group_rows, depth), rows_map),
        pl.BlockSpec((depth, tile), columns_map),
    ]
    operands = [info, rows, weight]
    if base is not None:
        in_specs.append(piece)
        operands.append(base)
    shape = (group_rows, chunk)
    outs = [jax.ShapeDtypeStruct(shape, jnp.bfloat16)]
    if with_total:
        outs += [jax.ShapeDtypeStruct(shape, jnp.bfloat16), jax.ShapeDtypeStruct(shape, jnp.float32)]

    def live(row):
        return index(row) < count

    return chain.call(
        functools.partial(piece_kernel, live, base is not None, with_total),
        in_specs,
        operands,
        prefetch=1,
        grid=(tiles,),
        out_specs=[piece] * len(outs),
        out_shape=outs,
        cost=(2 * group_rows * depth * chunk, 2 * depth * (chunk + group_rows) + 8 * group_rows * chunk),
    )


def choose_kernel(ends, info, here_ref, there_ref, out_ref):
    out_ref[...] = jnp.where(ends(info[0]), here_ref[...], there_ref[...])


def choose(chain, info, ends, here, there):
    size, chunk = here.shape
    tile = chunk // 2 if chunk % 256 == 0 else chunk
    piece = pl.BlockSpec((size, tile), lambda t, info: (0, t))
    return chain.call(
        functools.partial(choose_kernel, ends),
        [piece, piece],
        [info, here, there],
        prefetch=1,
        grid=(chunk // tile,),
        out_specs=[piece],
        out_shape=[jax.ShapeDtypeStruct(here.shape, here.dtype)],
        cost=(0, 6 * size * chunk),
    )[0]


def mix_kernel(groups, unit, info, ours_at, theirs_at, *refs):
    theirs, slopes = refs[:groups], refs[groups : 2 * groups]
    outs = refs[2 * groups : 3 * groups]
    their_rows, slope_rows = refs[3 * groups :]
    size = theirs[0].shape[0]
    for g in range(groups):
        their_rows[g * size : (g + 1) * size, :] = theirs[g][...]
        slope_rows[g * size : (g + 1) * size, :] = slopes[g][...]
    for k in range(groups * size // unit):
        a = their_rows[pl.ds(pl.multiple_of(theirs_at[k] * unit, unit), unit), :].astype(jnp.float32)
        b = slope_rows[pl.ds(pl.multiple_of(ours_at[k] * unit, unit), unit), :]
        where = k // groups * unit
        outs[k % groups][where : where + unit, :] = (a * b).astype(jnp.bfloat16)


def mix(chain, info, ours_at, theirs_at, theirs, slopes, unit):
    groups = len(theirs)
    size, chunk = theirs[0].shape
    tile = min(256, tile_of(chunk))
    piece = pl.BlockSpec((size, tile), lambda t, *_: (0, t))
    return chain.call(
        functools.partial(mix_kernel, groups, unit),
        [piece] * (2 * groups),
        [info, ours_at, theirs_at, *theirs, *slopes],
        prefetch=3,
        grid=(chunk // tile,),
        out_specs=[piece] * groups,
        out_shape=[jax.ShapeDtypeStruct((size, chunk), jnp.bfloat16)] * groups,
        cost=(0, 8 * groups * size * chunk),
        scratch=[
            pltpu.VMEM((groups * size, tile), jnp.bfloat16),
            pltpu.VMEM((groups * size, tile), jnp.float32),
        ],
    )


def product_kernel(hops, members, with_base, info, *refs):
    out_ref = refs[-1]
    values = refs[: hops * members]
    lower_ref, upper_ref = refs[hops * members : hops * members + 2]
    step, row, last = pl.program_id(0), info[0], hops - 1
    size = values[0].shape[0]
    dims = (((1,), (1,)), ((), ()))
    for m in range(members):
        stages = values[m * hops : (m + 1) * hops]
        upper_value, lower_value = stages[0][...], stages[last][...]
        for d in range(1, last + 1):
            upper_value = jnp.where(row == d, stages[d][...], upper_value)
            lower_value = jnp.where(row == d, stages[last - d][...], lower_value)
        term = lax.dot_general(lower_value, lower_ref[...], dims, preferred_element_type=jnp.float32)
        term += lax.dot_general(upper_value, upper_ref[...], dims, preferred_element_type=jnp.float32)
        here = pl.ds(m * size, size)

        @pl.when(step == 0)
        def _(term=term, here=here):
            out_ref[here, :] = term + refs[-2][here, :] if with_base else term

        @pl.when(step > 0)
        def _(term=term, here=here):
            out_ref[here, :] += term


def product_sum(chain, info, stages, weight, base, base_at, j, chunks):
    members, hops = len(stages), len(stages[0])
    size, chunk = stages[0][0].shape
    depth = weight.shape[0]
    tile = tile_of(chunk)
    tiles = chunk // tile
    piece = pl.BlockSpec((size, tile), lambda t, info: (0, t))
    in_specs = [piece] * (members * hops)
    in_specs += [
        pl.BlockSpec((depth, tile), lambda t, info: (0, j * tiles + t)),
        pl.BlockSpec((depth, tile), lambda t, info: (0, (chunks + j) * tiles + t)),
    ]
    operands = [info, *[value for member in stages for value in member], weight, weight]
    if base is not None:
        in_specs.append(pl.BlockSpec((members * size, depth), lambda t, info: (base_at, 0)))
        operands.append(base)
    return chain.call(
        functools.partial(product_kernel, hops, members, base is not None),
        in_specs,
        operands,
        prefetch=1,
        grid=(tiles,),
        out_specs=[pl.BlockSpec((members * size, depth), lambda t, info: (0, 0))],
        out_shape=[jax.ShapeDtypeStruct((members * size, depth), jnp.float32)],
        cost=(4 * members * size * depth * chunk, 4 * depth * chunk + 8 * members * size * depth),
    )[0]


def per_device(streams, tiles, order):
    row_size, col_size = lax.axis_size("row"), lax.axis_size("col")
    row, col = lax.axis_index("row"), lax.axis_index("col")
    section = lax.axis_index("section")
    bits = col_size.bit_length() - 1
    own_rows, weight = streams[0], tiles[0]
    local, depth = own_rows.shape
    tokens = local * col_size
    chunks, groups = COLUMN_CHUNKS, TOKEN_GROUPS
    group_rows = tokens // groups
    unit = local // groups
    last = row_size - 1
    info = jnp.stack([row, section]).astype(jnp.int32)

    each = col_size // groups
    per_block = tokens // order.shape[0] // unit
    counter = jnp.arange(order.shape[0], dtype=jnp.int32)
    inverse = jnp.sum(jnp.where(order[None, :] == counter[:, None], counter[None, :], 0), axis=1)
    moved = jnp.where(section == 0, inverse, order)
    units = jnp.arange(tokens // unit, dtype=jnp.int32)
    source = (moved[:, None] * per_block + jnp.arange(per_block, dtype=jnp.int32)).reshape(-1)

    def position(index):
        shard, found = (index // groups) ^ col, 0
        for bit in range(bits):
            found = found | (((shard >> bit) & 1) << (bits - 1 - bit))
        return (found * groups + index % groups).astype(jnp.int32)

    ours_at, theirs_at = position(units), position(source)

    even = [(d, d ^ 1) for d in range(row_size)]
    odd = [(d, ((d - 1) ^ 1) + 1) for d in range(1, last)]
    count = groups * chunks
    pieces = [(0, j) for j in range(chunks)]
    pieces += [(g, j) for j in range(chunks) for g in range(1, groups)]
    span = 3 * (row_size - 2) // 2
    ready = [max(i for i, (_, k) in enumerate(pieces) if k == j) for j in range(chunks)]
    sends = [(t, j) for j in range(chunks) for t in range(groups)]
    back = max(ready[j] + span + 4 - i for i, (_, j) in enumerate(sends))
    back = max(back, count)
    final = back + count - 1
    even_slots = final + span + 1
    odd_slots = range(1, final + 2 + 3 * (row_size - 4) // 2)

    def first_index(slot, r):
        q = jnp.where(r % 2 == 1, r, last - r)
        return slot - 3 * ((q - 1) // 2)

    def second_index(slot, r):
        q = jnp.where(r % 2 == 0, r, last - r)
        return slot + 2 - 3 * (q // 2)

    def first_half(r):
        return 1 - r % 2

    def second_half(r):
        return r % 2

    def gathered(later):
        shards, masks = gather_rows(own_rows, bits, later)
        if each > 1:
            shards = [jnp.concatenate(shards[i * each : (i + 1) * each]) for i in range(groups)]
        return jnp.stack(shards)

    def rows_for(newest):
        if each == 1 and newest < chunks:
            return own_rows[None]
        if not whole_rows:
            whole_rows.append(gathered(chain.value if chain.value is not None else own_rows))
        return whole_rows[0]

    def at_end(r):
        return (r == 0) | (r == last)

    def is_live(index):
        return 0 <= index < count

    chain, whole_rows = Chain(), []
    even_send, odd_send, even_got, odd_got = {}, {}, {}, {}
    incoming, slopes, mixed, waiting = {}, {}, {}, []
    sums, finished = {}, [None] * groups

    def second(slot):
        base = odd_got.get(slot)
        newest = slot + 2
        if 0 <= newest - back < count:
            value = mixed[sends[newest - back]]
            base = value if base is None else choose(chain, info, at_end, value, base)
        if any(is_live(newest - 3 * (q // 2)) for q in range(0, last, 2)):
            (base,) = piece_sum(
                chain, info, rows_for(newest), weight, base,
                functools.partial(second_index, slot), second_half, count, chunks, False,
            )
        even_send[newest] = base

    def first(slot):
        base = even_got[slot]
        if slot - 2 - span in incoming:
            chain.watch.append(incoming[slot - 2 - span])
        total = is_live(slot - span)
        passes = any(is_live(slot - 3 * ((q - 1) // 2)) for q in range(1, last, 2))
        odd_send[slot + 1] = base
        if total or passes:
            send, *rest = piece_sum(
                chain, info, rows_for(slot), weight, base,
                functools.partial(first_index, slot), first_half, count, chunks, total,
            )
            if passes:
                odd_send[slot + 1] = send
            if total:
                outgoing, slopes[slot - span] = rest
                incoming[slot - span] = partner(outgoing, "section", 0)

    second(-2)
    second(-1)
    even_got[0] = lax.ppermute(even_send[0], "row", even)
    for slot in range(even_slots):
        if slot + 1 < even_slots:
            even_got[slot + 1] = lax.ppermute(even_send[slot + 1], "row", even)
        first(slot)
        if slot + 1 in odd_slots:
            odd_got[slot + 1] = lax.ppermute(odd_send[slot + 1], "row", odd)
        for j in range(chunks):
            if slot == ready[j] + span + 2:
                found = [pieces.index((g, j)) for g in range(groups)]
                parts = mix(
                    chain, info, ours_at, theirs_at, [incoming[i] for i in found], [slopes[i] for i in found], unit
                )
                mixed.update({(t, j): part for t, part in enumerate(parts)})
        b = slot - span - back
        if b >= 0:
            t, j = sends[b]
            index = back + b
            stages = [mixed[(t, j)]]
            for q in range(1, row_size):
                if q % 2 == 1:
                    stages.append(even_got[index + 3 * ((q - 1) // 2)])
                else:
                    stages.append(odd_got[index - 2 + 3 * (q // 2)])
            waiting.append(stages)
            if j < chunks - 1 and t % 2 == 1:
                sums[t // 2] = product_sum(chain, info, waiting, weight, sums.get(t // 2), 0, j, chunks)
                waiting = []
            if j == chunks - 1:
                parts = product_sum(chain, info, waiting, weight, sums[t // 2], t % 2, j, chunks)
                waiting = []
                parts = parts.reshape(col_size, unit, depth)
                finished[t] = scatter_sum(parts, col, bits).astype(jnp.bfloat16)
        if slot + 2 < even_slots:
            second(slot)
    return jnp.concatenate(finished)[None]


def solution(mesh):
    placed = (P("section", "col", "row"), P("section", "row", "col"), P())
    return jax.shard_map(
        per_device,
        mesh=mesh,
        in_specs=placed,
        out_specs=P("section", "col", "row"),
        check_vma=False,
    )
```

```python
import functools

import jax
import jax.numpy as jnp
from jax import lax
from jax.experimental import pallas as pl
from jax.experimental.pallas import tpu as pltpu
from jax.sharding import PartitionSpec as P

gelu_scale = 0.7978845608
gelu_cubic = 0.044715
COLUMN_CHUNKS = 3
TOKEN_GROUPS = 4
TILES = (512, 256, 128)
VMEM_BYTES = 47 * 2**20
COST = 0.3


def partner(value, axis, bit):
    mask = 2**bit
    pairs = [(source, source ^ mask) for source in range(lax.axis_size(axis))]
    return lax.ppermute(value, axis, pairs)


def gather_rows(own):
    size = lax.axis_size("col")
    shards = [own]
    for mask in range(1, size):
        pairs = [(source, source ^ mask) for source in range(size)]
        shards.append(lax.ppermute(own, "col", pairs))
    return shards


def tile_of(chunk):
    return next(tile for tile in TILES if chunk % tile == 0)


class Chain:
    def __init__(self):
        self.value = None
        self.watch = []

    def call(self, kernel, specs, operands, **kwargs):
        earlier = ([] if self.value is None else [self.value]) + self.watch
        extra, self.watch = len(earlier), []
        prefetch = kwargs["prefetch"]
        skip = prefetch + len(specs)

        def body(*refs):
            kernel(*refs[:skip], *refs[skip + extra :])

        outs = pl.pallas_call(
            body,
            grid_spec=pltpu.PrefetchScalarGridSpec(
                num_scalar_prefetch=prefetch,
                grid=kwargs["grid"],
                in_specs=specs + [pl.BlockSpec(memory_space=pl.ANY)] * extra,
                out_specs=kwargs["out_specs"],
                scratch_shapes=kwargs.get("scratch", ()),
            ),
            out_shape=kwargs["out_shape"],
            compiler_params=pltpu.CompilerParams(vmem_limit_bytes=VMEM_BYTES),
            cost_estimate=pl.CostEstimate(flops=int(COST * kwargs["cost"][0]) + 1, bytes_accessed=int(COST * kwargs["cost"][1]) + 1, transcendentals=0),
        )(*operands, *earlier)
        self.value = outs[0]
        return outs


def scatter_sum(partials, col, bits):
    held = partials
    for bit in range(bits):
        pairs = held.reshape(held.shape[0] // 2, 2, *held.shape[1:])
        mine = (col >> bit) & 1
        keep = jnp.where(mine == 0, pairs[:, 0], pairs[:, 1])
        give = jnp.where(mine == 0, pairs[:, 1], pairs[:, 0])
        if bit > 0:
            give = give.astype(jnp.bfloat16)
        held = keep + partner(give, "col", bit).astype(jnp.float32)
    return held[0]


def piece_of(index, chunks, groups):
    rest = jnp.maximum(index - chunks, 0)
    first = index < chunks
    group = jnp.where(first, 0, 1 + lax.rem(rest, groups - 1))
    return group, jnp.where(first, index, lax.div(rest, groups - 1))


def piece_kernel(live, with_base, with_total, info, rows_ref, columns_ref, *rest):
    if with_base:
        base_ref, *rest = rest
    send_ref = rest[0]
    sums = jnp.dot(rows_ref[0], columns_ref[...], preferred_element_type=jnp.float32)
    sums = jnp.where(live(info[0]), sums, 0.0)
    if with_base:
        sums = sums + base_ref[...].astype(jnp.float32)
    send_ref[...] = sums.astype(send_ref.dtype)
    if with_total:
        out_ref, slope_ref = rest[1:]

        @pl.when(info[1] == 0)
        def _():
            v = sums
            inner = jnp.tanh(gelu_scale * (v + gelu_cubic * v * v * v))
            out_ref[...] = (0.5 * v * (1.0 + inner)).astype(out_ref.dtype)
            slope_ref[...] = 0.5 * (1.0 + inner) + 0.5 * v * (1.0 - inner * inner) * gelu_scale * (
                1.0 + 3.0 * gelu_cubic * v * v
            )

        @pl.when(info[1] != 0)
        def _():
            out_ref[...] = sums.astype(out_ref.dtype)
            slope_ref[...] = jnp.ones_like(slope_ref)


def piece_sum(chain, info, rows, weight, base, index, upper, count, chunks, with_total):
    groups, group_rows, depth = rows.shape
    chunk = weight.shape[1] // (2 * chunks)
    tile = tile_of(chunk)
    tiles = chunk // tile

    def which(info):
        return piece_of(jnp.clip(index(info[0]), 0, count - 1), chunks, TOKEN_GROUPS)

    def rows_map(t, info):
        return (which(info)[0] if groups > 1 else 0, 0, 0)

    def columns_map(t, info):
        return (0, (upper(info[0]) * chunks + which(info)[1]) * tiles + t)

    piece = pl.BlockSpec((group_rows, tile), lambda t, info: (0, t))
    in_specs = [
        pl.BlockSpec((1, group_rows, depth), rows_map),
        pl.BlockSpec((depth, tile), columns_map),
    ]
    operands = [info, rows, weight]
    if base is not None:
        in_specs.append(piece)
        operands.append(base)
    shape = (group_rows, chunk)
    outs = [jax.ShapeDtypeStruct(shape, jnp.bfloat16)]
    if with_total:
        outs += [jax.ShapeDtypeStruct(shape, jnp.bfloat16), jax.ShapeDtypeStruct(shape, jnp.float32)]

    def live(row):
        return index(row) < count

    return chain.call(
        functools.partial(piece_kernel, live, base is not None, with_total),
        in_specs,
        operands,
        prefetch=1,
        grid=(tiles,),
        out_specs=[piece] * len(outs),
        out_shape=outs,
        cost=(2 * group_rows * depth * chunk, 2 * depth * (chunk + group_rows) + 8 * group_rows * chunk),
    )


def choose_kernel(ends, info, here_ref, there_ref, out_ref):
    out_ref[...] = jnp.where(ends(info[0]), here_ref[...], there_ref[...])


def choose(chain, info, ends, here, there):
    size, chunk = here.shape
    tile = chunk // 2 if chunk % 256 == 0 else chunk
    piece = pl.BlockSpec((size, tile), lambda t, info: (0, t))
    return chain.call(
        functools.partial(choose_kernel, ends),
        [piece, piece],
        [info, here, there],
        prefetch=1,
        grid=(chunk // tile,),
        out_specs=[piece],
        out_shape=[jax.ShapeDtypeStruct(here.shape, here.dtype)],
        cost=(0, 6 * size * chunk),
    )[0]


def mix_kernel(groups, unit, info, ours_at, theirs_at, *refs):
    theirs, slopes = refs[:groups], refs[groups : 2 * groups]
    outs = refs[2 * groups : 3 * groups]
    their_rows, slope_rows = refs[3 * groups :]
    size = theirs[0].shape[0]
    for g in range(groups):
        their_rows[g * size : (g + 1) * size, :] = theirs[g][...]
        slope_rows[g * size : (g + 1) * size, :] = slopes[g][...]
    for k in range(groups * size // unit):
        a = their_rows[pl.ds(pl.multiple_of(theirs_at[k] * unit, unit), unit), :].astype(jnp.float32)
        b = slope_rows[pl.ds(pl.multiple_of(ours_at[k] * unit, unit), unit), :]
        where = k // groups * unit
        outs[k % groups][where : where + unit, :] = (a * b).astype(jnp.bfloat16)


def mix(chain, info, ours_at, theirs_at, theirs, slopes, unit):
    groups = len(theirs)
    size, chunk = theirs[0].shape
    tile = min(256, tile_of(chunk))
    piece = pl.BlockSpec((size, tile), lambda t, *_: (0, t))
    return chain.call(
        functools.partial(mix_kernel, groups, unit),
        [piece] * (2 * groups),
        [info, ours_at, theirs_at, *theirs, *slopes],
        prefetch=3,
        grid=(chunk // tile,),
        out_specs=[piece] * groups,
        out_shape=[jax.ShapeDtypeStruct((size, chunk), jnp.bfloat16)] * groups,
        cost=(0, 8 * groups * size * chunk),
        scratch=[
            pltpu.VMEM((groups * size, tile), jnp.bfloat16),
            pltpu.VMEM((groups * size, tile), jnp.float32),
        ],
    )


def product_kernel(hops, members, with_base, info, *refs):
    out_ref = refs[-1]
    values = refs[: hops * members]
    lower_ref, upper_ref = refs[hops * members : hops * members + 2]
    step, row, last = pl.program_id(0), info[0], hops - 1
    size = values[0].shape[0]
    dims = (((1,), (1,)), ((), ()))
    for m in range(members):
        stages = values[m * hops : (m + 1) * hops]
        upper_value, lower_value = stages[0][...], stages[last][...]
        for d in range(1, last + 1):
            upper_value = jnp.where(row == d, stages[d][...], upper_value)
            lower_value = jnp.where(row == d, stages[last - d][...], lower_value)
        term = lax.dot_general(lower_value, lower_ref[...], dims, preferred_element_type=jnp.float32)
        term += lax.dot_general(upper_value, upper_ref[...], dims, preferred_element_type=jnp.float32)
        here = pl.ds(m * size, size)

        @pl.when(step == 0)
        def _(term=term, here=here):
            out_ref[here, :] = term + refs[-2][here, :] if with_base else term

        @pl.when(step > 0)
        def _(term=term, here=here):
            out_ref[here, :] += term


def product_sum(chain, info, stages, weight, base, base_at, j, chunks):
    members, hops = len(stages), len(stages[0])
    size, chunk = stages[0][0].shape
    depth = weight.shape[0]
    tile = tile_of(chunk)
    tiles = chunk // tile
    piece = pl.BlockSpec((size, tile), lambda t, info: (0, t))
    in_specs = [piece] * (members * hops)
    in_specs += [
        pl.BlockSpec((depth, tile), lambda t, info: (0, j * tiles + t)),
        pl.BlockSpec((depth, tile), lambda t, info: (0, (chunks + j) * tiles + t)),
    ]
    operands = [info, *[value for member in stages for value in member], weight, weight]
    if base is not None:
        in_specs.append(pl.BlockSpec((members * size, depth), lambda t, info: (base_at, 0)))
        operands.append(base)
    return chain.call(
        functools.partial(product_kernel, hops, members, base is not None),
        in_specs,
        operands,
        prefetch=1,
        grid=(tiles,),
        out_specs=[pl.BlockSpec((members * size, depth), lambda t, info: (0, 0))],
        out_shape=[jax.ShapeDtypeStruct((members * size, depth), jnp.float32)],
        cost=(4 * members * size * depth * chunk, 4 * depth * chunk + 8 * members * size * depth),
    )[0]


def per_device(streams, tiles, order):
    row_size, col_size = lax.axis_size("row"), lax.axis_size("col")
    row, col = lax.axis_index("row"), lax.axis_index("col")
    section = lax.axis_index("section")
    bits = col_size.bit_length() - 1
    own_rows, weight = streams[0], tiles[0]
    local, depth = own_rows.shape
    tokens = local * col_size
    chunks, groups = COLUMN_CHUNKS, TOKEN_GROUPS
    group_rows = tokens // groups
    unit = local // groups
    last = row_size - 1
    info = jnp.stack([row, section]).astype(jnp.int32)

    each = col_size // groups
    per_block = tokens // order.shape[0] // unit
    counter = jnp.arange(order.shape[0], dtype=jnp.int32)
    inverse = jnp.sum(jnp.where(order[None, :] == counter[:, None], counter[None, :], 0), axis=1)
    moved = jnp.where(section == 0, inverse, order)
    units = jnp.arange(tokens // unit, dtype=jnp.int32)
    source = (moved[:, None] * per_block + jnp.arange(per_block, dtype=jnp.int32)).reshape(-1)

    def position(index):
        shard = (index // groups) ^ col
        return (shard * groups + index % groups).astype(jnp.int32)

    ours_at, theirs_at = position(units), position(source)

    even = [(d, d ^ 1) for d in range(row_size)]
    odd = [(d, ((d - 1) ^ 1) + 1) for d in range(1, last)]
    count = groups * chunks
    pieces = [(0, j) for j in range(chunks)]
    pieces += [(g, j) for j in range(chunks) for g in range(1, groups)]
    span = 3 * (row_size - 2) // 2
    ready = [max(i for i, (_, k) in enumerate(pieces) if k == j) for j in range(chunks)]
    sends = [(t, j) for j in range(chunks) for t in range(groups)]
    back = max(ready[j] + span + 4 - i for i, (_, j) in enumerate(sends))
    back = max(back, count)
    final = back + count - 1
    even_slots = final + span + 1
    odd_slots = range(1, final + 2 + 3 * (row_size - 4) // 2)

    def first_index(slot, r):
        q = jnp.where(r % 2 == 1, r, last - r)
        return slot - 3 * ((q - 1) // 2)

    def second_index(slot, r):
        q = jnp.where(r % 2 == 0, r, last - r)
        return slot + 2 - 3 * (q // 2)

    def first_half(r):
        return 1 - r % 2

    def second_half(r):
        return r % 2

    def gathered():
        shards = gather_rows(own_rows)
        if each > 1:
            shards = [jnp.concatenate(shards[i * each : (i + 1) * each]) for i in range(groups)]
        return jnp.stack(shards)

    def rows_for(newest):
        if each == 1 and newest < chunks:
            return own_rows[None]
        if not whole_rows:
            whole_rows.append(gathered())
        return whole_rows[0]

    def at_end(r):
        return (r == 0) | (r == last)

    def is_live(index):
        return 0 <= index < count

    chain, whole_rows = Chain(), []
    even_send, odd_send, even_got, odd_got = {}, {}, {}, {}
    incoming, slopes, mixed = {}, {}, {}
    sums, finished = {}, [None] * groups

    def second(slot):
        base = odd_got.get(slot)
        newest = slot + 2
        if 0 <= newest - back < count:
            value = mixed[sends[newest - back]]
            base = value if base is None else choose(chain, info, at_end, value, base)
        if any(is_live(newest - 3 * (q // 2)) for q in range(0, last, 2)):
            (base,) = piece_sum(
                chain, info, rows_for(newest), weight, base,
                functools.partial(second_index, slot), second_half, count, chunks, False,
            )
        even_send[newest] = base

    def first(slot):
        base = even_got[slot]
        if slot - 2 - span in incoming:
            chain.watch.append(incoming[slot - 2 - span])
        total = is_live(slot - span)
        passes = any(is_live(slot - 3 * ((q - 1) // 2)) for q in range(1, last, 2))
        odd_send[slot + 1] = base
        if total or passes:
            send, *rest = piece_sum(
                chain, info, rows_for(slot), weight, base,
                functools.partial(first_index, slot), first_half, count, chunks, total,
            )
            if passes:
                odd_send[slot + 1] = send
            if total:
                outgoing, slopes[slot - span] = rest
                incoming[slot - span] = partner(outgoing, "section", 0)

    second(-2)
    second(-1)
    even_got[0] = lax.ppermute(even_send[0], "row", even)
    for slot in range(even_slots):
        if slot + 1 < even_slots:
            even_got[slot + 1] = lax.ppermute(even_send[slot + 1], "row", even)
        first(slot)
        if slot + 1 in odd_slots:
            odd_got[slot + 1] = lax.ppermute(odd_send[slot + 1], "row", odd)
        for j in range(chunks):
            if slot == ready[j] + span + 2:
                found = [pieces.index((g, j)) for g in range(groups)]
                parts = mix(
                    chain, info, ours_at, theirs_at, [incoming[i] for i in found], [slopes[i] for i in found], unit
                )
                mixed.update({(t, j): part for t, part in enumerate(parts)})
        b = slot - span - back
        if b >= 0:
            t, j = sends[b]
            index = back + b
            stages = [mixed[(t, j)]]
            for q in range(1, row_size):
                if q % 2 == 1:
                    stages.append(even_got[index + 3 * ((q - 1) // 2)])
                else:
                    stages.append(odd_got[index - 2 + 3 * (q // 2)])
            sums[t] = product_sum(chain, info, [stages], weight, sums.get(t), 0, j, chunks)
            if j == chunks - 1:
                parts = sums[t]
                parts = parts.reshape(col_size, unit, depth)
                finished[t] = scatter_sum(parts, col, bits).astype(jnp.bfloat16)
        if slot + 2 < even_slots:
            second(slot)
    return jnp.concatenate(finished)[None]


def solution(mesh):
    placed = (P("section", "col", "row"), P("section", "row", "col"), P())
    return jax.shard_map(
        per_device,
        mesh=mesh,
        in_specs=placed,
        out_specs=P("section", "col", "row"),
        check_vma=False,
    )
```

```python
import functools

import jax
import jax.numpy as jnp
from jax import lax
from jax.experimental import pallas as pl
from jax.experimental.pallas import tpu as pltpu
from jax.sharding import PartitionSpec as P

gelu_scale = 0.7978845608
gelu_cubic = 0.044715
COLUMN_CHUNKS = 3
TOKEN_GROUPS = 4
TILES = (512, 256, 128)
VMEM_BYTES = 47 * 2**20
COST = 0.3


def partner(value, axis, bit):
    mask = 2**bit
    pairs = [(source, source ^ mask) for source in range(lax.axis_size(axis))]
    return lax.ppermute(value, axis, pairs)


def gather_rows(own):
    size = lax.axis_size("col")
    shards = [own]
    for mask in range(1, size):
        pairs = [(source, source ^ mask) for source in range(size)]
        shards.append(lax.ppermute(own, "col", pairs))
    return shards


def tile_of(chunk):
    return next(tile for tile in TILES if chunk % tile == 0)


class Chain:
    def __init__(self):
        self.value = None
        self.watch = []

    def call(self, kernel, specs, operands, **kwargs):
        earlier = ([] if self.value is None else [self.value]) + self.watch
        extra, self.watch = len(earlier), []
        prefetch = kwargs["prefetch"]
        skip = prefetch + len(specs)

        def body(*refs):
            kernel(*refs[:skip], *refs[skip + extra :])

        outs = pl.pallas_call(
            body,
            grid_spec=pltpu.PrefetchScalarGridSpec(
                num_scalar_prefetch=prefetch,
                grid=kwargs["grid"],
                in_specs=specs + [pl.BlockSpec(memory_space=pl.ANY)] * extra,
                out_specs=kwargs["out_specs"],
                scratch_shapes=kwargs.get("scratch", ()),
            ),
            out_shape=kwargs["out_shape"],
            compiler_params=pltpu.CompilerParams(vmem_limit_bytes=VMEM_BYTES),
            cost_estimate=pl.CostEstimate(flops=int(COST * kwargs["cost"][0]) + 1, bytes_accessed=int(COST * kwargs["cost"][1]) + 1, transcendentals=0),
        )(*operands, *earlier)
        self.value = outs[0]
        return outs


def scatter_sum(partials, col, bits, given):
    held = partials
    for bit in range(bits):
        pairs = held.reshape(held.shape[0] // 2, 2, *held.shape[1:])
        mine = (col >> bit) & 1
        keep = jnp.where(mine == 0, pairs[:, 0], pairs[:, 1])
        give = jnp.where(mine == 0, pairs[:, 1], pairs[:, 0])
        if bit > 0:
            give = give.astype(jnp.bfloat16)
        given.append(give)
        held = keep + partner(give, "col", bit).astype(jnp.float32)
    return held[0]


def piece_of(index, chunks, groups):
    rest = jnp.maximum(index - chunks, 0)
    first = index < chunks
    group = jnp.where(first, 0, 1 + lax.rem(rest, groups - 1))
    return group, jnp.where(first, index, lax.div(rest, groups - 1))


def piece_kernel(live, with_base, with_total, info, rows_ref, columns_ref, *rest):
    if with_base:
        base_ref, *rest = rest
    send_ref = rest[0]
    sums = jnp.dot(rows_ref[0], columns_ref[...], preferred_element_type=jnp.float32)
    sums = jnp.where(live(info[0]), sums, 0.0)
    if with_base:
        sums = sums + base_ref[...].astype(jnp.float32)
    send_ref[...] = sums.astype(send_ref.dtype)
    if with_total:
        out_ref, slope_ref = rest[1:]

        @pl.when(info[1] == 0)
        def _():
            v = sums
            inner = jnp.tanh(gelu_scale * (v + gelu_cubic * v * v * v))
            out_ref[...] = (0.5 * v * (1.0 + inner)).astype(out_ref.dtype)
            slope_ref[...] = 0.5 * (1.0 + inner) + 0.5 * v * (1.0 - inner * inner) * gelu_scale * (
                1.0 + 3.0 * gelu_cubic * v * v
            )

        @pl.when(info[1] != 0)
        def _():
            out_ref[...] = sums.astype(out_ref.dtype)
            slope_ref[...] = jnp.ones_like(slope_ref)


def piece_sum(chain, info, rows, weight, base, index, upper, count, chunks, with_total):
    groups, group_rows, depth = rows.shape
    chunk = weight.shape[1] // (2 * chunks)
    tile = tile_of(chunk)
    tiles = chunk // tile

    def which(info):
        return piece_of(jnp.clip(index(info[0]), 0, count - 1), chunks, TOKEN_GROUPS)

    def rows_map(t, info):
        return (which(info)[0] if groups > 1 else 0, 0, 0)

    def columns_map(t, info):
        return (0, (upper(info[0]) * chunks + which(info)[1]) * tiles + t)

    piece = pl.BlockSpec((group_rows, tile), lambda t, info: (0, t))
    in_specs = [
        pl.BlockSpec((1, group_rows, depth), rows_map),
        pl.BlockSpec((depth, tile), columns_map),
    ]
    operands = [info, rows, weight]
    if base is not None:
        in_specs.append(piece)
        operands.append(base)
    shape = (group_rows, chunk)
    outs = [jax.ShapeDtypeStruct(shape, jnp.bfloat16)]
    if with_total:
        outs += [jax.ShapeDtypeStruct(shape, jnp.bfloat16), jax.ShapeDtypeStruct(shape, jnp.float32)]

    def live(row):
        return index(row) < count

    return chain.call(
        functools.partial(piece_kernel, live, base is not None, with_total),
        in_specs,
        operands,
        prefetch=1,
        grid=(tiles,),
        out_specs=[piece] * len(outs),
        out_shape=outs,
        cost=(2 * group_rows * depth * chunk, 2 * depth * (chunk + group_rows) + 8 * group_rows * chunk),
    )


def choose_kernel(ends, info, here_ref, there_ref, out_ref):
    out_ref[...] = jnp.where(ends(info[0]), here_ref[...], there_ref[...])


def choose(chain, info, ends, here, there):
    size, chunk = here.shape
    tile = chunk // 2 if chunk % 256 == 0 else chunk
    piece = pl.BlockSpec((size, tile), lambda t, info: (0, t))
    return chain.call(
        functools.partial(choose_kernel, ends),
        [piece, piece],
        [info, here, there],
        prefetch=1,
        grid=(chunk // tile,),
        out_specs=[piece],
        out_shape=[jax.ShapeDtypeStruct(here.shape, here.dtype)],
        cost=(0, 6 * size * chunk),
    )[0]


def mix_kernel(groups, unit, info, ours_at, theirs_at, *refs):
    theirs, slopes = refs[:groups], refs[groups : 2 * groups]
    outs = refs[2 * groups : 3 * groups]
    their_rows, slope_rows = refs[3 * groups :]
    size = theirs[0].shape[0]
    for g in range(groups):
        their_rows[g * size : (g + 1) * size, :] = theirs[g][...]
        slope_rows[g * size : (g + 1) * size, :] = slopes[g][...]
    for k in range(groups * size // unit):
        a = their_rows[pl.ds(pl.multiple_of(theirs_at[k] * unit, unit), unit), :].astype(jnp.float32)
        b = slope_rows[pl.ds(pl.multiple_of(ours_at[k] * unit, unit), unit), :]
        where = k // groups * unit
        outs[k % groups][where : where + unit, :] = (a * b).astype(jnp.bfloat16)


def mix(chain, info, ours_at, theirs_at, theirs, slopes, unit):
    groups = len(theirs)
    size, chunk = theirs[0].shape
    tile = min(256, tile_of(chunk))
    piece = pl.BlockSpec((size, tile), lambda t, *_: (0, t))
    return chain.call(
        functools.partial(mix_kernel, groups, unit),
        [piece] * (2 * groups),
        [info, ours_at, theirs_at, *theirs, *slopes],
        prefetch=3,
        grid=(chunk // tile,),
        out_specs=[piece] * groups,
        out_shape=[jax.ShapeDtypeStruct((size, chunk), jnp.bfloat16)] * groups,
        cost=(0, 8 * groups * size * chunk),
        scratch=[
            pltpu.VMEM((groups * size, tile), jnp.bfloat16),
            pltpu.VMEM((groups * size, tile), jnp.float32),
        ],
    )


def product_kernel(hops, members, with_base, info, *refs):
    out_ref = refs[-1]
    values = refs[: hops * members]
    lower_ref, upper_ref = refs[hops * members : hops * members + 2]
    step, row, last = pl.program_id(0), info[0], hops - 1
    size = values[0].shape[0]
    dims = (((1,), (1,)), ((), ()))
    for m in range(members):
        stages = values[m * hops : (m + 1) * hops]
        upper_value, lower_value = stages[0][...], stages[last][...]
        for d in range(1, last + 1):
            upper_value = jnp.where(row == d, stages[d][...], upper_value)
            lower_value = jnp.where(row == d, stages[last - d][...], lower_value)
        term = lax.dot_general(lower_value, lower_ref[...], dims, preferred_element_type=jnp.float32)
        term += lax.dot_general(upper_value, upper_ref[...], dims, preferred_element_type=jnp.float32)
        here = pl.ds(m * size, size)

        @pl.when(step == 0)
        def _(term=term, here=here):
            out_ref[here, :] = term + refs[-2][here, :] if with_base else term

        @pl.when(step > 0)
        def _(term=term, here=here):
            out_ref[here, :] += term


def product_sum(chain, info, stages, weight, base, base_at, j, chunks):
    members, hops = len(stages), len(stages[0])
    size, chunk = stages[0][0].shape
    depth = weight.shape[0]
    tile = tile_of(chunk)
    tiles = chunk // tile
    piece = pl.BlockSpec((size, tile), lambda t, info: (0, t))
    in_specs = [piece] * (members * hops)
    in_specs += [
        pl.BlockSpec((depth, tile), lambda t, info: (0, j * tiles + t)),
        pl.BlockSpec((depth, tile), lambda t, info: (0, (chunks + j) * tiles + t)),
    ]
    operands = [info, *[value for member in stages for value in member], weight, weight]
    if base is not None:
        in_specs.append(pl.BlockSpec((members * size, depth), lambda t, info: (base_at, 0)))
        operands.append(base)
    return chain.call(
        functools.partial(product_kernel, hops, members, base is not None),
        in_specs,
        operands,
        prefetch=1,
        grid=(tiles,),
        out_specs=[pl.BlockSpec((members * size, depth), lambda t, info: (0, 0))],
        out_shape=[jax.ShapeDtypeStruct((members * size, depth), jnp.float32)],
        cost=(4 * members * size * depth * chunk, 4 * depth * chunk + 8 * members * size * depth),
    )[0]


def per_device(streams, tiles, order):
    row_size, col_size = lax.axis_size("row"), lax.axis_size("col")
    row, col = lax.axis_index("row"), lax.axis_index("col")
    section = lax.axis_index("section")
    bits = col_size.bit_length() - 1
    own_rows, weight = streams[0], tiles[0]
    local, depth = own_rows.shape
    tokens = local * col_size
    chunks, groups = COLUMN_CHUNKS, TOKEN_GROUPS
    group_rows = tokens // groups
    unit = local // groups
    last = row_size - 1
    info = jnp.stack([row, section]).astype(jnp.int32)

    each = col_size // groups
    per_block = tokens // order.shape[0] // unit
    counter = jnp.arange(order.shape[0], dtype=jnp.int32)
    inverse = jnp.sum(jnp.where(order[None, :] == counter[:, None], counter[None, :], 0), axis=1)
    moved = jnp.where(section == 0, inverse, order)
    units = jnp.arange(tokens // unit, dtype=jnp.int32)
    source = (moved[:, None] * per_block + jnp.arange(per_block, dtype=jnp.int32)).reshape(-1)

    def position(index):
        shard = (index // groups) ^ col
        return (shard * groups + index % groups).astype(jnp.int32)

    ours_at, theirs_at = position(units), position(source)

    even = [(d, d ^ 1) for d in range(row_size)]
    odd = [(d, ((d - 1) ^ 1) + 1) for d in range(1, last)]
    count = groups * chunks
    pieces = [(0, j) for j in range(chunks)]
    pieces += [(g, j) for j in range(chunks) for g in range(1, groups)]
    span = 3 * (row_size - 2) // 2
    ready = [max(i for i, (_, k) in enumerate(pieces) if k == j) for j in range(chunks)]
    sends = [(t, j) for j in range(chunks) for t in range(groups)]
    back = max(ready[j] + span + 4 - i for i, (_, j) in enumerate(sends))
    back = max(back, count)
    final = back + count - 1
    even_slots = final + span + 1
    odd_slots = range(1, final + 2 + 3 * (row_size - 4) // 2)

    def first_index(slot, r):
        q = jnp.where(r % 2 == 1, r, last - r)
        return slot - 3 * ((q - 1) // 2)

    def second_index(slot, r):
        q = jnp.where(r % 2 == 0, r, last - r)
        return slot + 2 - 3 * (q // 2)

    def first_half(r):
        return 1 - r % 2

    def second_half(r):
        return r % 2

    def gathered():
        shards = gather_rows(own_rows)
        if each > 1:
            shards = [jnp.concatenate(shards[i * each : (i + 1) * each]) for i in range(groups)]
        return jnp.stack(shards)

    def rows_for(newest):
        if each == 1 and newest < chunks:
            return own_rows[None]
        if not whole_rows:
            whole_rows.append(gathered())
        return whole_rows[0]

    def at_end(r):
        return (r == 0) | (r == last)

    def is_live(index):
        return 0 <= index < count

    chain, whole_rows = Chain(), []
    even_send, odd_send, even_got, odd_got = {}, {}, {}, {}
    incoming, slopes, mixed = {}, {}, {}
    sums, finished, given = {}, [None] * groups, [[] for _ in range(groups)]

    def second(slot):
        base = odd_got.get(slot)
        newest = slot + 2
        if 0 <= newest - back < count:
            value = mixed[sends[newest - back]]
            base = value if base is None else choose(chain, info, at_end, value, base)
        if any(is_live(newest - 3 * (q // 2)) for q in range(0, last, 2)):
            (base,) = piece_sum(
                chain, info, rows_for(newest), weight, base,
                functools.partial(second_index, slot), second_half, count, chunks, False,
            )
        even_send[newest] = base

    def first(slot):
        base = even_got[slot]
        if slot - 2 - span in incoming:
            chain.watch.append(incoming[slot - 2 - span])
        total = is_live(slot - span)
        passes = any(is_live(slot - 3 * ((q - 1) // 2)) for q in range(1, last, 2))
        odd_send[slot + 1] = base
        if total or passes:
            send, *rest = piece_sum(
                chain, info, rows_for(slot), weight, base,
                functools.partial(first_index, slot), first_half, count, chunks, total,
            )
            if passes:
                odd_send[slot + 1] = send
            if total:
                outgoing, slopes[slot - span] = rest
                incoming[slot - span] = partner(outgoing, "section", 0)

    second(-2)
    second(-1)
    even_got[0] = lax.ppermute(even_send[0], "row", even)
    for slot in range(even_slots):
        if slot + 1 < even_slots:
            even_got[slot + 1] = lax.ppermute(even_send[slot + 1], "row", even)
        first(slot)
        if slot + 1 in odd_slots:
            odd_got[slot + 1] = lax.ppermute(odd_send[slot + 1], "row", odd)
        for j in range(chunks):
            if slot == ready[j] + span + 2:
                found = [pieces.index((g, j)) for g in range(groups)]
                parts = mix(
                    chain, info, ours_at, theirs_at, [incoming[i] for i in found], [slopes[i] for i in found], unit
                )
                mixed.update({(t, j): part for t, part in enumerate(parts)})
        b = slot - span - back
        if b >= 0:
            t, j = sends[b]
            index = back + b
            stages = [mixed[(t, j)]]
            for q in range(1, row_size):
                if q % 2 == 1:
                    stages.append(even_got[index + 3 * ((q - 1) // 2)])
                else:
                    stages.append(odd_got[index - 2 + 3 * (q // 2)])
            if t >= 2 and j == chunks - 1:
                chain.watch.append(given[t - 2][-1])
            sums[t] = product_sum(chain, info, [stages], weight, sums.get(t), 0, j, chunks)
            if j == chunks - 1:
                parts = sums[t]
                parts = parts.reshape(col_size, unit, depth)
                finished[t] = scatter_sum(parts, col, bits, given[t]).astype(jnp.bfloat16)
        if slot + 2 < even_slots:
            second(slot)
    return jnp.concatenate(finished)[None]


def solution(mesh):
    placed = (P("section", "col", "row"), P("section", "row", "col"), P())
    return jax.shard_map(
        per_device,
        mesh=mesh,
        in_specs=placed,
        out_specs=P("section", "col", "row"),
        check_vma=False,
    )
```
